512 devices in a mesh: region: 16 (over z_hi, y), worker: 32 (over z_lo, x, core).
Axes of the slice: x: 4, y: 8, z: 8 (z_hi: 2, z_lo: 4; z = z_hi * 4 + z_lo), core: 2. Of those that a mesh axis runs over, the one named last changes fastest.
Arguments:
- worker_start: bfloat16 [16, 128, 4096], P('region'), may hold values from -0.5 to 0.5
- inputs: bfloat16 [16, 32, 4, 256, 128], P('region', 'worker'), may hold values from -6 to 6
- teacher: bfloat16 [128, 4096], replicated, may hold values from -0.5 to 0.5
- regional_momentum: float32 [16, 128, 4096], P('region', 'worker'), may hold values from -1.5 to 1.5
- global_params: float32 [128, 4096], P('worker', 'region'), may hold values from -6 to 6
- global_momentum: float32 [128, 4096], P('worker', 'region'), may hold values from -1.5 to 1.5
- staleness: int32 [16], replicated, may hold values from 0 to 4
- arrival_order: int32 [16], replicated, may hold values from 0 to 15, as said below
- pull_slot: int32 [16], replicated, may hold values from 0 to 15, as said below
Outputs:
- momentum_regional: float32 [16, 128, 4096], P('region', 'worker')
- params_global: float32 [128, 4096], P('worker', 'region')
- momentum_global: float32 [128, 4096], P('worker', 'region')
- worker_params: float32 [16, 128, 4096], P('region')
The draws below stay inside these ranges and needn't reach their ends.
Inputs may be any that keep to these rules, and one draw needn't show every extreme that they name: arrival_order is a permutation of the regions 0 .. 15. pull_slot[r] is at least the position of region r in arrival_order; the region that arrives first has slot 0.
All inputs are finite; a program needn't handle non-finite values.
Results may differ from the reference program's by a relative error of at most 0.00043.
Values sent between devices are 32-bit elements; how exact they have to be, the bound alone decides.
A program may use at most 64 MiB of HBM per device.

```python
import jax
import jax.numpy as jnp
from jax import lax

D = 4096
ROWS = 128
TOK = 256
STEPS = 4
REGIONS = 16
WORKERS = 32


def arrival_plan(key):
    arrival = jax.random.permutation(jax.random.fold_in(key, 31), REGIONS).astype(jnp.int32)
    position = jnp.argsort(arrival).astype(jnp.int32)
    extra = jax.random.randint(jax.random.fold_in(key, 37), (REGIONS,), 0, REGIONS - position).astype(jnp.int32)
    slots = jnp.where(position == 0, 0, position + extra).astype(jnp.int32)
    return (arrival, slots)


def draw_arrival_order(key, part):
    return arrival_plan(key)[0]


def draw_pull_slot(key, part):
    return arrival_plan(key)[1]


def set_ends(result, key, least, high):
    longest = result.shape.index(max(result.shape))
    spots = []
    for shift in (0, 1):
        where = [jax.random.randint(jax.random.fold_in(key, axis), (), 0, length) for axis, length in enumerate(result.shape)]
        where[longest] = (where[longest] + shift) % result.shape[longest]
        spots.append(tuple(where))
    return result.at[spots[0]].set(least).at[spots[1]].set(high)


def block_scale(rng, dims, shards, least, top_value):
    loudness, own = 1.0, jax.random.fold_in(rng, 6)
    for axis_at, shards_of in shards:
        draws = jnp.exp(jax.random.uniform(jax.random.fold_in(own, axis_at), (shards_of,), jnp.float32, least / len(shards), top_value / len(shards)))
        loudness = loudness * jnp.repeat(draws, dims[axis_at] // shards_of).reshape([-1 if axis == axis_at else 1 for axis in range(len(dims))])
    return loudness


def gaussian(rng, extent, deviation, reach, shards=(), held_as=jnp.bfloat16):
    level = block_scale(rng, extent, shards, -0.22, 0.18) if shards else 1.0
    drawn = jax.random.normal(rng, extent, jnp.float32) * deviation * level
    return jnp.minimum(jnp.maximum(drawn, -reach), reach).astype(held_as)


def setup_inputs(seed: int = 0) -> dict:
    arg_keys = jax.random.split(jax.random.key(seed), 10)
    return {
        "worker_start": gaussian(arg_keys[0], (REGIONS, ROWS, D), ROWS ** -0.5, 0.5, ((0, 16),)),
        "inputs": gaussian(arg_keys[1], (REGIONS, WORKERS, STEPS, TOK, ROWS), 1.0, 6.0, ((0, 16), (1, 32))),
        "teacher": gaussian(arg_keys[2], (ROWS, D), ROWS ** -0.5, 0.5),
        "regional_momentum": gaussian(arg_keys[3], (REGIONS, ROWS, D), 0.1, 1.5, ((0, 16), (1, 32)), jnp.float32),
        "global_params": gaussian(arg_keys[4], (ROWS, D), 0.5, 6.0, ((0, 32), (1, 16)), jnp.float32),
        "global_momentum": gaussian(arg_keys[5], (ROWS, D), 0.1, 1.5, ((0, 32), (1, 16)), jnp.float32),
        "staleness": set_ends(jax.random.randint(arg_keys[6], (REGIONS,), 0, 5), jax.random.fold_in(arg_keys[6], 1), 0, 4).astype(jnp.int32),
        "arrival_order": draw_arrival_order(jax.random.fold_in(arg_keys[9], 71), 0),
        "pull_slot": draw_pull_slot(jax.random.fold_in(arg_keys[9], 71), 0),
    }


LOCAL_RATE = 0.3
REGION_BETA = 0.9
REGION_RATE = 1.0
GLOBAL_MU = 0.9
GLOBAL_RATE = 0.7


def residual_of(weights, micro_batch, teacher):
    target = jax.nn.silu(jnp.dot(micro_batch, teacher, preferred_element_type=jnp.float32))
    predicted = jnp.dot(micro_batch, weights.astype(jnp.bfloat16), preferred_element_type=jnp.float32)
    return (predicted - target).astype(jnp.bfloat16)


def gradient_of(micro_batch, residual):
    return lax.dot_general(micro_batch, residual, (((0,), (0,)), ((), ())), preferred_element_type=jnp.float32)


def pseudo_gradient(initial, hidden, teacher):
    start_weights = initial.astype(jnp.float32)
    step_scale = LOCAL_RATE / hidden.shape[1]
    current = start_weights
    for local_step in range(hidden.shape[0]):
        residual = residual_of(current, hidden[local_step], teacher)
        current = current - step_scale * gradient_of(hidden[local_step], residual)
    return start_weights - current


def reference(worker_start, inputs, teacher, regional_momentum, global_params, global_momentum, staleness, arrival_order, pull_slot):
    def one_region(region_args):
        initial, region_inputs, momentum = region_args

        def add_worker(total, worker_inputs):
            pseudo = pseudo_gradient(initial, worker_inputs, teacher)
            return total + pseudo, None

        summed, unused = lax.scan(add_worker, jnp.zeros(initial.shape, jnp.float32), region_inputs)
        momentum_new = REGION_BETA * momentum + summed / WORKERS
        return momentum_new, REGION_RATE * momentum_new

    momentum_regional, deltas = lax.map(one_region, (worker_start, inputs, regional_momentum))
    weights = 1.0 / (1.0 + staleness.astype(jnp.float32))

    def advance(state_pair, arrival):
        params_now, momentum_now = state_pair
        source = arrival_order[arrival]
        update = weights[source] * deltas[source]
        momentum_now = GLOBAL_MU * momentum_now + update
        params_now = params_now - GLOBAL_RATE * (update + GLOBAL_MU * momentum_now)
        return (params_now, momentum_now), params_now

    (params_global, momentum_global), versions = lax.scan(advance, (global_params, global_momentum), jnp.arange(REGIONS, dtype=jnp.int32))
    pulled = versions[pull_slot]
    return momentum_regional, params_global, momentum_global, pulled
```

```python
import jax
import jax.numpy as jnp
from jax import lax
from jax.experimental import pallas as pl
from jax.experimental.pallas import tpu as pltpu
from jax.sharding import PartitionSpec as P

LOCAL_RATE = 0.3
REGION_BETA = 0.9
REGION_RATE = 1.0
GLOBAL_MU = 0.9
GLOBAL_RATE = 0.7

MESH = pl.DeviceIdType.MESH
F32 = jnp.float32
BF16 = jnp.bfloat16

NZ = 4
NX = 4
H = 256

LAG_A, LAG_B, LAG_C, LAG_D, LAG_E, LAG_F, LAG_G, LAG_H = 1, 2, 2, 2, 2, 2, 2, 1
A, B, C, D, E, F, G, HH = range(8)


def dot(a, b):
    return jnp.dot(a, b, preferred_element_type=F32)


def kernel(
    nr,
    stale_ref,
    order_ref,
    slot_ref,
    x_hbm,
    t_hbm,
    w_hbm,
    mom_hbm,
    par_hbm,
    gmom_hbm,
    mom_hout,
    par_hout,
    gmom_hout,
    wp_hout,
    out_mom,
    out_pm,
    out_wp,
    x_v,
    xt_v,
    t_v,
    w_v,
    s_other,
    s_own,
    r_a,
    r_b,
    s_c,
    r_c,
    d_all,
    d_now,
    weights,
    f_all,
    pm_all,
    pm_oth,
    mo_own,
    mo_oth,
    mo_send,
    g_send,
    x_sem,
    t_sem,
    w_sem,
    mo_sem,
    pm_sem,
    send,
    recv,
    misc_send,
    misc_recv,
    mo_ssem,
    mo_rsem,
    out_sem,
):
    nc = nr // 2
    ny = nr // 2
    steps, tokens, _ = x_v.shape
    scale = LOCAL_RATE / tokens
    workers = NZ * NX * 2
    r = lax.axis_index("region")
    w = lax.axis_index("worker")
    z = w // (NX * 2)
    x = (w // 2) % NX
    c = w % 2

    def wid(zz, xx, cc):
        return (zz * NX + xx) * 2 + cc

    partner = {"worker": wid(z, x, 1 - c)}
    x_of = [(x + i) % NX for i in range(NX)]
    z_of = [(z + i) % NZ for i in range(NZ)]
    x_peer = [{"worker": wid(z, x_of[i], c)} for i in range(NX)]
    z_peer = [{"worker": wid(z_of[i], x, c)} for i in range(NZ)]
    hi = r // ny
    y = r % ny
    hi_peer = {"region": (1 - hi) * ny + y}
    y_peer = [{"region": hi * ny + (y + i) % ny} for i in range(ny)]

    barrier = pltpu.get_barrier_semaphore()
    peers = [partner, hi_peer] + x_peer[1:] + z_peer[1:] + y_peer[1:]
    for peer in peers:
        pl.semaphore_signal(barrier, inc=1, device_id=peer, device_id_type=MESH)

    def put(src, dst, s_sem, r_sem, peer):
        pltpu.make_async_remote_copy(
            src_ref=src, dst_ref=dst, send_sem=s_sem, recv_sem=r_sem, device_id=peer, device_id_type=MESH
        ).start()

    def take(ref, sem):
        pltpu.make_async_copy(ref, ref, sem).wait()

    pltpu.make_async_copy(x_hbm.at[0, 0], x_v, x_sem).start()
    for k in range(nc):
        cols = pl.ds(k * 2 * H, 2 * H)
        pltpu.make_async_copy(t_hbm.at[:, cols], t_v.at[k], t_sem.at[k]).start()
        pltpu.make_async_copy(w_hbm.at[0, :, cols], w_v.at[k], w_sem.at[k]).start()
    for k in range(nc):
        mine = pl.ds(pl.multiple_of((2 * k + c) * H, H), H)
        pltpu.make_async_copy(mom_hbm.at[0, :, mine], mo_own.at[k], mo_sem.at[k]).start()
    pltpu.make_async_copy(par_hbm, pm_all.at[0, 0, 0, 0], pm_sem.at[0]).start()
    pltpu.make_async_copy(gmom_hbm, pm_all.at[0, 0, 0, 1], pm_sem.at[1]).start()

    pltpu.make_async_copy(x_hbm.at[0, 0], x_v, x_sem).wait()
    for s in range(steps):
        xt_v[s] = x_v[s].T
    for i in range(nr):
        weights[i] = 1.0 / (1.0 + jnp.full((8, H), stale_ref[i].astype(F32)))

    def tile(k, half):
        cols = pl.ds(pl.multiple_of(half * H, H), H)
        teach = t_v[k, :, cols].T
        start = w_v[k, :, cols].T.astype(F32)
        now = start
        for s in range(steps):
            v = dot(teach, xt_v[s])
            predicted = dot(now.astype(BF16), xt_v[s])
            residual = (predicted - v * jax.nn.sigmoid(v)).astype(BF16)
            now = now - scale * dot(residual, x_v[s])
        return (start - now).T.reshape(NZ, NX, 8, H)

    def compute(k):
        cols = pl.ds(0, 2 * H)
        pltpu.make_async_copy(t_hbm.at[:, cols], t_v.at[k], t_sem.at[k]).wait()
        pltpu.make_async_copy(w_hbm.at[0, :, cols], w_v.at[k], w_sem.at[k]).wait()
        s_other[k] = tile(k, 1 - c)
        s_own[k] = tile(k, c)

    def send_a(k):
        put(s_other.at[k], r_a.at[k], send.at[A, k], recv.at[A, k], partner)

    def opening():
        pl.semaphore_wait(barrier, len(peers))
        put(par_hbm, pm_all.at[0, 0, 1, 0], misc_send.at[0], misc_recv.at[0], hi_peer)
        put(gmom_hbm, pm_all.at[0, 0, 1, 1], misc_send.at[0], misc_recv.at[0], hi_peer)
        for k in range(nc):
            theirs = pl.ds(pl.multiple_of((2 * k + 1 - c) * H, H), H)
            put(mom_hbm.at[0, :, theirs], mo_oth.at[k], mo_ssem.at[0, k], mo_rsem.at[0, k], partner)
        send_a(0)

    def stage_b(k):
        take(r_a.at[k], recv.at[A, k])
        s_own[k] = s_own[k] + r_a[k]
        for i in range(1, NX):
            put(s_own.at[k, :, x_of[i]], r_b.at[k, i - 1], send.at[B, k], recv.at[B, k], x_peer[i])

    def stage_c(k):
        take(r_b.at[k], recv.at[B, k])
        total = s_own[k, :, x]
        for i in range(NX - 1):
            total = total + r_b[k, i]
        s_c[k] = total
        for i in range(1, NZ):
            put(s_c.at[k, z_of[i]], r_c.at[k, i - 1], send.at[C, k], recv.at[C, k], z_peer[i])

    def both(mine, other):
        low = jnp.where(c == 0, mine, other)
        high = jnp.where(c == 0, other, mine)
        return jnp.concatenate([low, high], axis=0)

    def parts(value):
        low, high = value[:4], value[4:]
        return jnp.where(c == 0, low, high), jnp.where(c == 0, high, low)

    def columns(k):
        return pl.ds(pl.multiple_of((2 * k + c) * H, H), H)

    def stage_d(k):
        take(mo_own.at[k], mo_sem.at[k])
        take(mo_oth.at[k], mo_rsem.at[0, k])
        take(r_c.at[k], recv.at[C, k])
        summed = s_c[k, z]
        for i in range(NZ - 1):
            summed = summed + r_c[k, i]
        momentum = REGION_BETA * both(mo_own[k], mo_oth[k]) + summed / workers
        d_all[k, 0, 0] = REGION_RATE * momentum
        put(d_all.at[k, 0, 0], d_all.at[k, 0, 1], send.at[D, k], recv.at[D, k], hi_peer)
        mine, other = parts(momentum)
        out_mom[k, c] = mine
        mo_send[k] = other
        put(mo_send.at[k], out_mom.at[k, c], mo_ssem.at[1, k], mo_rsem.at[1, k], partner)

    def stage_e(k):
        take(d_all.at[k, 0, 1], recv.at[D, k])
        for i in range(1, ny):
            put(d_all.at[k, 0], d_all.at[k, i], send.at[E, k], recv.at[E, k], y_peer[i])

    def spread():
        take(par_hbm, pm_sem.at[0])
        take(gmom_hbm, pm_sem.at[1])
        take(pm_all.at[0, 0, 1], misc_recv.at[0])
        for i in range(1, ny):
            put(pm_all.at[0, 0], pm_all.at[i // 2, i % 2], misc_send.at[1], misc_recv.at[1], y_peer[i])

    def exchange():
        take(d_all.at[0, pl.ds(1, ny - 1)], misc_recv.at[1])
        put(pm_all.at[:, (y + 1 - c) % 2], pm_oth, misc_send.at[2], misc_recv.at[2], partner)

    def stage_f(k):
        take(d_all.at[k, pl.ds(1, ny - 1)], recv.at[E, k])
        for i in range(ny):
            for h in range(2):
                source = ((hi + h) % 2) * ny + (y - i + ny) % ny
                d_now[source] = weights[source] * d_all[k, i, h]
        owner = 2 * k + c
        away = (y - owner % ny + ny) % ny
        side = (owner // ny + hi) % 2
        params = both(pm_all[away // 2, away % 2, side, 0], pm_oth[away // 2, side, 0])
        momentum = both(pm_all[away // 2, away % 2, side, 1], pm_oth[away // 2, side, 1])
        slot = slot_ref[r]
        pulled = params
        for arrival in range(nr):
            update = d_now[order_ref[arrival]]
            momentum = GLOBAL_MU * momentum + update
            params = params - GLOBAL_RATE * (update + GLOBAL_MU * momentum)
            pulled = jnp.where(slot == arrival, params, pulled)
        f_all[k, z] = pulled
        for i in range(1, NZ):
            put(f_all.at[k, z], f_all.at[k, z], send.at[F, k], recv.at[F, k], z_peer[i])

        @pl.when(2 * k + c == r)
        def _():
            for i, value in enumerate((params, momentum)):
                mine, other = parts(value)
                out_pm[i] = mine
                g_send[i] = other
            put(g_send, out_pm, misc_send.at[3], misc_recv.at[3], partner)

    def stage_g(k):
        take(f_all.at[k, pl.ds(0, NZ - 1)], recv.at[F, k])
        out_wp[:, x, :, columns(k)] = f_all[k]
        for i in range(1, NX):
            put(f_all.at[k], out_wp.at[:, x, :, columns(k)], send.at[G, k], recv.at[G, k], x_peer[i])

    def stage_h(k):
        take(r_b.at[k], recv.at[G, k])
        put(out_wp.at[:, :, :, columns(k)], out_wp.at[:, :, :, columns(k)], send.at[HH, k], recv.at[HH, k], partner)

    def stage_end(k):
        take(r_a.at[k], recv.at[HH, k])
        take(mo_oth.at[k], mo_rsem.at[1, k])
        chunk = pl.ds(pl.multiple_of(2 * k * H, 2 * H), 2 * H)
        pltpu.make_async_copy(out_wp.at[:, :, :, chunk], wp_hout.at[:, :, :, chunk], out_sem.at[0, k]).start()
        for i in range(2):
            half = pl.ds(pl.multiple_of((2 * k + i) * H, H), H)
            pltpu.make_async_copy(out_mom.at[k, i], mom_hout.at[0, :, half], out_sem.at[1 + i, k]).start()
        take(r_a.at[k], send.at[A, k])
        take(r_b.at[k], send.at[B, k])
        take(r_c.at[k], send.at[C, k])
        take(d_all.at[k, 0, 1], send.at[D, k])
        take(d_all.at[k, pl.ds(1, ny - 1)], send.at[E, k])
        take(f_all.at[k, pl.ds(0, NZ - 1)], send.at[F, k])
        take(r_b.at[k], send.at[G, k])
        take(r_a.at[k], send.at[HH, k])
        take(mo_oth.at[k], mo_ssem.at[0, k])
        take(mo_oth.at[k], mo_ssem.at[1, k])

    at_b = LAG_A
    at_c = at_b + LAG_B
    at_d = at_c + LAG_C
    at_e = at_d + LAG_D
    at_f = at_e + LAG_E
    at_g = at_f + LAG_F
    at_h = at_g + LAG_G
    at_end = at_h + LAG_H

    def tick(t, _):
        def when(lag, stage):
            @pl.when((t >= lag) & (t < nc + lag))
            def _():
                stage(t - lag)

        when(0, compute)
        pl.when(t == 1)(opening)

        @pl.when((t >= 1) & (t < nc))
        def _():
            send_a(t)

        when(at_end, stage_end)
        when(at_h, stage_h)
        when(at_g, stage_g)
        pl.when(t == 3)(spread)
        pl.when(t == at_f - 1)(exchange)

        @pl.when(t == at_f)
        def _():
            take(pm_oth, misc_recv.at[2])

        when(at_f, stage_f)
        when(at_e, stage_e)
        when(at_d, stage_d)
        when(at_c, stage_c)
        when(at_b, stage_b)
        return 0

    lax.fori_loop(0, nc + at_end, tick, 0)
    take(pm_all.at[0, 0, 1], misc_send.at[0])
    take(d_all.at[0, pl.ds(1, ny - 1)], misc_send.at[1])
    take(pm_oth, misc_send.at[2])

    @pl.when(r % 2 == c)
    def _():
        take(g_send, misc_send.at[3])

    @pl.when(r % 2 != c)
    def _():
        take(g_send, misc_recv.at[3])

    pltpu.make_async_copy(out_pm.at[0], par_hout, pm_sem.at[0]).start()
    pltpu.make_async_copy(out_pm.at[1], gmom_hout, pm_sem.at[1]).start()

    def written(k, _):
        take(out_wp.at[:, :, :, pl.ds(0, 2 * H)], out_sem.at[0, k])
        take(mo_send.at[k], out_sem.at[1, k])
        take(mo_send.at[k], out_sem.at[2, k])
        return 0

    lax.fori_loop(0, nc, written, 0)
    take(out_pm.at[0], pm_sem.at[0])
    take(out_pm.at[1], pm_sem.at[1])


def hand_on(mom, par, gmom, wp, mom_out, par_out, gmom_out, wp_out):
    mom_out[...] = mom[...]
    par_out[...] = par[...]
    gmom_out[...] = gmom[...]
    wp_out[...] = wp[...]


def local(nr, worker_start, inputs, teacher, regional_momentum, global_params, global_momentum, staleness, arrival_order, pull_slot):
    _, _, steps, tokens, rows = inputs.shape
    nc = nr // 2
    width = 2 * H
    smem = pl.BlockSpec(memory_space=pltpu.SMEM)
    hbm = pl.BlockSpec(memory_space=pltpu.HBM)
    dma = pltpu.SemaphoreType.DMA
    shapes = (
        jax.ShapeDtypeStruct((1, 4, nc * width), F32),
        jax.ShapeDtypeStruct((4, H), F32),
        jax.ShapeDtypeStruct((4, H), F32),
        jax.ShapeDtypeStruct((NZ, NX, 8, nc * width), F32),
    )
    results = pl.pallas_call(
        lambda *refs: kernel(nr, *refs),
        out_shape=shapes,
        in_specs=[smem] * 3 + [hbm] * 6,
        out_specs=(hbm,) * 4,
        scratch_shapes=[
            pltpu.VMEM((nc, 2, 4, H), F32),
            pltpu.VMEM((2, 4, H), F32),
            pltpu.VMEM((NZ, NX, 8, nc * width), F32),
            pltpu.VMEM((steps, tokens, rows), BF16),
            pltpu.VMEM((steps, rows, tokens), BF16),
            pltpu.VMEM((nc, rows, width), BF16),
            pltpu.VMEM((nc, rows, width), BF16),
            pltpu.VMEM((nc, NZ, NX, 8, H), F32),
            pltpu.VMEM((nc, NZ, NX, 8, H), F32),
            pltpu.VMEM((nc, NZ, NX, 8, H), F32),
            pltpu.VMEM((nc, NX - 1, NZ, 8, H), F32),
            pltpu.VMEM((nc, NZ, 8, H), F32),
            pltpu.VMEM((nc, NZ - 1, 8, H), F32),
            pltpu.VMEM((nc, nr // 2, 2, 8, H), F32),
            pltpu.VMEM((nr, 8, H), F32),
            pltpu.VMEM((nr, 8, H), F32),
            pltpu.VMEM((nc, NZ, 8, H), F32),
            pltpu.VMEM((nr // 4, 2, 2, 2, 4, H), F32),
            pltpu.VMEM((nr // 4, 2, 2, 4, H), F32),
            pltpu.VMEM((nc, 4, H), F32),
            pltpu.VMEM((nc, 4, H), F32),
            pltpu.VMEM((nc, 4, H), F32),
            pltpu.VMEM((2, 4, H), F32),
            dma,
            dma((nc,)),
            dma((nc,)),
            dma((nc,)),
            dma((2,)),
            dma((8, nc)),
            dma((8, nc)),
            dma((4,)),
            dma((4,)),
            dma((2, nc)),
            dma((2, nc)),
            dma((3, nc)),
        ],
        compiler_params=pltpu.CompilerParams(
            collective_id=0, has_side_effects=True, vmem_limit_bytes=60 * 2**20
        ),
        cost_estimate=pl.CostEstimate(flops=3300000000, bytes_accessed=5000000, transcendentals=4000000),
        name="outer_step",
    )(
        staleness,
        arrival_order,
        pull_slot,
        inputs,
        teacher,
        worker_start,
        regional_momentum,
        global_params,
        global_momentum,
    )
    whole = [pl.BlockSpec(shape.shape, lambda i, n=len(shape.shape): (0,) * n) for shape in shapes[:3]]
    whole.append(pl.BlockSpec((1, NX, 8, nc * width), lambda i: (i, 0, 0, 0)))
    out_mom, out_par, out_gmom, out_wp = pl.pallas_call(
        hand_on,
        grid=(NZ,),
        out_shape=shapes,
        in_specs=whole,
        out_specs=tuple(whole),
        compiler_params=pltpu.CompilerParams(vmem_limit_bytes=60 * 2**20),
        name="hand_on",
    )(*results)
    return out_mom, out_par, out_gmom, out_wp.reshape(1, rows, nc * width)


def solution(mesh):
    nr = mesh.shape["region"]
    placed = (
        P("region", None, None),
        P("region", "worker", None, None, None),
        P(),
        P("region", "worker", None),
        P("worker", "region"),
        P("worker", "region"),
        P(),
        P(),
        P(),
    )
    return jax.shard_map(
        lambda *args: local(nr, *args),
        mesh=mesh,
        in_specs=placed,
        out_specs=(
            P("region", "worker", None),
            P("worker", "region"),
            P("worker", "region"),
            P("region", None, None),
        ),
        check_vma=False,
    )
```

```python
import jax
import jax.numpy as jnp
from jax import lax
from jax.experimental import pallas as pl
from jax.experimental.pallas import tpu as pltpu
from jax.sharding import PartitionSpec as P

LOCAL_RATE = 0.3
REGION_BETA = 0.9
REGION_RATE = 1.0
GLOBAL_MU = 0.9
GLOBAL_RATE = 0.7

MESH = pl.DeviceIdType.MESH
F32 = jnp.float32
BF16 = jnp.bfloat16

NZ = 4
NX = 4
H = 256

PACE = 2
LAG_A, LAG_B, LAG_C, LAG_D, LAG_E, LAG_F, LAG_G, LAG_H = 2, 4, 4, 5, 7, 4, 4, 2
A, B, C, D, E, F, G, HH = range(8)


def dot(a, b):
    return jnp.dot(a, b, preferred_element_type=F32)


def kernel(
    nr,
    stale_ref,
    order_ref,
    slot_ref,
    x_hbm,
    t_hbm,
    w_hbm,
    mom_hbm,
    par_hbm,
    gmom_hbm,
    mom_hout,
    par_hout,
    gmom_hout,
    wp_hout,
    out_mom,
    out_pm,
    out_wp,
    x_v,
    xt_v,
    t_v,
    w_v,
    s_all,
    r_a,
    r_b,
    s_c,
    r_c,
    d_all,
    d_now,
    weights,
    f_all,
    pm_all,
    pm_oth,
    mo_own,
    mo_oth,
    mo_send,
    g_send,
    x_sem,
    t_sem,
    w_sem,
    mo_sem,
    pm_sem,
    send,
    recv,
    misc_send,
    misc_recv,
    mo_ssem,
    mo_rsem,
    out_sem,
):
    nc = nr // 2
    ny = nr // 2
    steps, tokens, _ = x_v.shape
    scale = LOCAL_RATE / tokens
    workers = NZ * NX * 2
    r = lax.axis_index("region")
    w = lax.axis_index("worker")
    z = w // (NX * 2)
    x = (w // 2) % NX
    c = w % 2

    def wid(zz, xx, cc):
        return (zz * NX + xx) * 2 + cc

    partner = {"worker": wid(z, x, 1 - c)}
    x_of = [(x + i) % NX for i in range(NX)]
    z_of = [(z + i) % NZ for i in range(NZ)]
    x_peer = [{"worker": wid(z, x_of[i], c)} for i in range(NX)]
    z_peer = [{"worker": wid(z_of[i], x, c)} for i in range(NZ)]
    hi = r // ny
    y = r % ny
    hi_peer = {"region": (1 - hi) * ny + y}
    y_peer = [{"region": hi * ny + (y + i) % ny} for i in range(ny)]

    barrier = pltpu.get_barrier_semaphore()
    peers = [partner, hi_peer] + x_peer[1:] + z_peer[1:] + y_peer[1:]
    for peer in peers:
        pl.semaphore_signal(barrier, inc=1, device_id=peer, device_id_type=MESH)

    def put(src, dst, s_sem, r_sem, peer):
        pltpu.make_async_remote_copy(
            src_ref=src, dst_ref=dst, send_sem=s_sem, recv_sem=r_sem, device_id=peer, device_id_type=MESH
        ).start()

    def take(ref, sem):
        pltpu.make_async_copy(ref, ref, sem).wait()

    pltpu.make_async_copy(x_hbm.at[0, 0], x_v, x_sem).start()
    for k in range(nc):
        cols = pl.ds(k * 2 * H, 2 * H)
        pltpu.make_async_copy(t_hbm.at[:, cols], t_v.at[k], t_sem.at[k]).start()
        pltpu.make_async_copy(w_hbm.at[0, :, cols], w_v.at[k], w_sem.at[k]).start()
    for k in range(nc):
        mine = pl.ds(pl.multiple_of((2 * k + c) * H, H), H)
        pltpu.make_async_copy(mom_hbm.at[0, :, mine], mo_own.at[k], mo_sem.at[k]).start()
    pltpu.make_async_copy(par_hbm, pm_all.at[0, 0, 0, 0], pm_sem.at[0]).start()
    pltpu.make_async_copy(gmom_hbm, pm_all.at[0, 0, 0, 1], pm_sem.at[1]).start()

    pltpu.make_async_copy(x_hbm.at[0, 0], x_v, x_sem).wait()
    for s in range(steps):
        xt_v[s] = x_v[s].T
    for i in range(nr):
        weights[i] = 1.0 / (1.0 + jnp.full((8, H), stale_ref[i].astype(F32)))

    def tile(k):
        teach = t_v[k].T
        start = w_v[k].T.astype(F32)
        now = start
        for s in range(steps):
            v = dot(teach, xt_v[s])
            predicted = dot(now.astype(BF16), xt_v[s])
            residual = (predicted - v * jax.nn.sigmoid(v)).astype(BF16)
            now = now - scale * dot(residual, x_v[s])
        return (start - now).T

    def compute(k):
        cols = pl.ds(0, 2 * H)
        pltpu.make_async_copy(t_hbm.at[:, cols], t_v.at[k], t_sem.at[k]).wait()
        pltpu.make_async_copy(w_hbm.at[0, :, cols], w_v.at[k], w_sem.at[k]).wait()
        pseudo = tile(k)
        for half in range(2):
            s_all[k, half] = pseudo[:, half * H : half * H + H].reshape(NZ, NX, 8, H)

    def send_a(k):
        put(s_all.at[k, 1 - c], r_a.at[k], send.at[A, k], recv.at[A, k], partner)

    def opening():
        pl.semaphore_wait(barrier, len(peers))
        put(par_hbm, pm_all.at[0, 0, 1, 0], misc_send.at[0], misc_recv.at[0], hi_peer)
        put(gmom_hbm, pm_all.at[0, 0, 1, 1], misc_send.at[0], misc_recv.at[0], hi_peer)
        for k in range(nc):
            theirs = pl.ds(pl.multiple_of((2 * k + 1 - c) * H, H), H)
            put(mom_hbm.at[0, :, theirs], mo_oth.at[k], mo_ssem.at[0, k], mo_rsem.at[0, k], partner)

    def stage_b(k):
        take(r_a.at[k], recv.at[A, k])
        s_all[k, c] = s_all[k, c] + r_a[k]
        for i in range(1, NX):
            put(s_all.at[k, c, :, x_of[i]], r_b.at[k, i - 1], send.at[B, k], recv.at[B, k], x_peer[i])

    def stage_c(k):
        take(r_b.at[k], recv.at[B, k])
        total = s_all[k, c, :, x]
        for i in range(NX - 1):
            total = total + r_b[k, i]
        s_c[k] = total
        for i in range(1, NZ):
            put(s_c.at[k, z_of[i]], r_c.at[k, i - 1], send.at[C, k], recv.at[C, k], z_peer[i])

    def both(mine, other):
        low = jnp.where(c == 0, mine, other)
        high = jnp.where(c == 0, other, mine)
        return jnp.concatenate([low, high], axis=0)

    def parts(value):
        low, high = value[:4], value[4:]
        return jnp.where(c == 0, low, high), jnp.where(c == 0, high, low)

    def columns(k):
        return pl.ds(pl.multiple_of((2 * k + c) * H, H), H)

    def stage_d(k):
        take(mo_own.at[k], mo_sem.at[k])
        take(mo_oth.at[k], mo_rsem.at[0, k])
        take(r_c.at[k], recv.at[C, k])
        summed = s_c[k, z]
        for i in range(NZ - 1):
            summed = summed + r_c[k, i]
        momentum = REGION_BETA * both(mo_own[k], mo_oth[k]) + summed / workers
        d_all[k, 0, 0] = REGION_RATE * momentum
        put(d_all.at[k, 0, 0], d_all.at[k, 0, 1], send.at[D, k], recv.at[D, k], hi_peer)
        mine, other = parts(momentum)
        out_mom[k, c] = mine
        mo_send[k] = other
        put(mo_send.at[k], out_mom.at[k, c], mo_ssem.at[1, k], mo_rsem.at[1, k], partner)

    def stage_e(k):
        take(d_all.at[k, 0, 1], recv.at[D, k])
        for i in range(1, ny):
            put(d_all.at[k, 0], d_all.at[k, i], send.at[E, k], recv.at[E, k], y_peer[i])

    def spread():
        take(par_hbm, pm_sem.at[0])
        take(gmom_hbm, pm_sem.at[1])
        take(pm_all.at[0, 0, 1], misc_recv.at[0])
        for i in range(1, ny):
            put(pm_all.at[0, 0], pm_all.at[i // 2, i % 2], misc_send.at[1], misc_recv.at[1], y_peer[i])

    def exchange():
        take(d_all.at[0, pl.ds(1, ny - 1)], misc_recv.at[1])
        put(pm_all.at[:, (y + 1 - c) % 2], pm_oth, misc_send.at[2], misc_recv.at[2], partner)

    def stage_f(k):
        take(d_all.at[k, pl.ds(1, ny - 1)], recv.at[E, k])
        for i in range(ny):
            for h in range(2):
                source = ((hi + h) % 2) * ny + (y - i + ny) % ny
                d_now[source] = weights[source] * d_all[k, i, h]
        owner = 2 * k + c
        away = (y - owner % ny + ny) % ny
        side = (owner // ny + hi) % 2
        params = both(pm_all[away // 2, away % 2, side, 0], pm_oth[away // 2, side, 0])
        momentum = both(pm_all[away // 2, away % 2, side, 1], pm_oth[away // 2, side, 1])
        slot = slot_ref[r]
        pulled = params
        for arrival in range(nr):
            update = d_now[order_ref[arrival]]
            momentum = GLOBAL_MU * momentum + update
            params = params - GLOBAL_RATE * (update + GLOBAL_MU * momentum)
            pulled = jnp.where(slot == arrival, params, pulled)
        f_all[k, z] = pulled
        for i in range(1, NZ):
            put(f_all.at[k, z], f_all.at[k, z], send.at[F, k], recv.at[F, k], z_peer[i])

        @pl.when(2 * k + c == r)
        def _():
            for i, value in enumerate((params, momentum)):
                mine, other = parts(value)
                out_pm[i] = mine
                g_send[i] = other
            put(g_send, out_pm, misc_send.at[3], misc_recv.at[3], partner)

    def stage_g(k):
        take(f_all.at[k, pl.ds(0, NZ - 1)], recv.at[F, k])
        out_wp[:, x, :, columns(k)] = f_all[k]
        for i in range(1, NX):
            put(f_all.at[k], out_wp.at[:, x, :, columns(k)], send.at[G, k], recv.at[G, k], x_peer[i])

    def stage_h(k):
        take(r_b.at[k], recv.at[G, k])
        put(out_wp.at[:, :, :, columns(k)], out_wp.at[:, :, :, columns(k)], send.at[HH, k], recv.at[HH, k], partner)

    def stage_end(k):
        take(r_a.at[k], recv.at[HH, k])
        take(mo_oth.at[k], mo_rsem.at[1, k])
        chunk = pl.ds(pl.multiple_of(2 * k * H, 2 * H), 2 * H)
        pltpu.make_async_copy(out_wp.at[:, :, :, chunk], wp_hout.at[:, :, :, chunk], out_sem.at[0, k]).start()
        for i in range(2):
            half = pl.ds(pl.multiple_of((2 * k + i) * H, H), H)
            pltpu.make_async_copy(out_mom.at[k, i], mom_hout.at[0, :, half], out_sem.at[1 + i, k]).start()
        take(r_a.at[k], send.at[A, k])
        take(r_b.at[k], send.at[B, k])
        take(r_c.at[k], send.at[C, k])
        take(d_all.at[k, 0, 1], send.at[D, k])
        take(d_all.at[k, pl.ds(1, ny - 1)], send.at[E, k])
        take(f_all.at[k, pl.ds(0, NZ - 1)], send.at[F, k])
        take(r_b.at[k], send.at[G, k])
        take(r_a.at[k], send.at[HH, k])
        take(mo_oth.at[k], mo_ssem.at[0, k])
        take(mo_oth.at[k], mo_ssem.at[1, k])

    at_b = LAG_A
    at_c = at_b + LAG_B
    at_d = at_c + LAG_C
    at_e = at_d + LAG_D
    at_f = at_e + LAG_E
    at_g = at_f + LAG_F
    at_h = at_g + LAG_G
    at_end = at_h + LAG_H

    def tick(t, _):
        def when(lag, stage):
            @pl.when((t >= lag) & (t < PACE * nc + lag) & ((t - lag) % PACE == 0))
            def _():
                stage((t - lag) // PACE)

        when(0, compute)
        pl.when(t == 0)(opening)
        when(0, send_a)
        when(at_end, stage_end)
        when(at_h, stage_h)
        when(at_g, stage_g)
        pl.when(t == 8)(spread)
        pl.when(t == at_f - 3)(exchange)

        @pl.when(t == at_f)
        def _():
            take(pm_oth, misc_recv.at[2])

        when(at_f, stage_f)
        when(at_e, stage_e)
        when(at_d, stage_d)
        when(at_c, stage_c)
        when(at_b, stage_b)
        return 0

    lax.fori_loop(0, PACE * (nc - 1) + at_end + 1, tick, 0)
    take(pm_all.at[0, 0, 1], misc_send.at[0])
    take(d_all.at[0, pl.ds(1, ny - 1)], misc_send.at[1])
    take(pm_oth, misc_send.at[2])

    @pl.when(r % 2 == c)
    def _():
        take(g_send, misc_send.at[3])

    @pl.when(r % 2 != c)
    def _():
        take(g_send, misc_recv.at[3])

    pltpu.make_async_copy(out_pm.at[0], par_hout, pm_sem.at[0]).start()
    pltpu.make_async_copy(out_pm.at[1], gmom_hout, pm_sem.at[1]).start()

    def written(k, _):
        take(out_wp.at[:, :, :, pl.ds(0, 2 * H)], out_sem.at[0, k])
        take(mo_send.at[k], out_sem.at[1, k])
        take(mo_send.at[k], out_sem.at[2, k])
        return 0

    lax.fori_loop(0, nc, written, 0)
    take(out_pm.at[0], pm_sem.at[0])
    take(out_pm.at[1], pm_sem.at[1])


def hand_on(*refs):
    given, made, held, arrive, leave = refs[:4], refs[4:8], refs[8:12], refs[12], refs[13]
    routes = [(given[3].at[i], held[3].at[i], made[3].at[i]) for i in range(NZ)]
    routes += [(given[i], held[i], made[i]) for i in range(3)]
    inward = [pltpu.make_async_copy(src, mid, arrive.at[i]) for i, (src, mid, _) in enumerate(routes)]
    outward = [pltpu.make_async_copy(mid, dst, leave.at[i]) for i, (_, mid, dst) in enumerate(routes)]
    for copy in inward:
        copy.start()
    for copy, onward in zip(inward, outward):
        copy.wait()
        onward.start()
    for copy in outward:
        copy.wait()


def local(nr, worker_start, inputs, teacher, regional_momentum, global_params, global_momentum, staleness, arrival_order, pull_slot):
    _, _, steps, tokens, rows = inputs.shape
    nc = nr // 2
    width = 2 * H
    smem = pl.BlockSpec(memory_space=pltpu.SMEM)
    hbm = pl.BlockSpec(memory_space=pltpu.HBM)
    dma = pltpu.SemaphoreType.DMA
    shapes = (
        jax.ShapeDtypeStruct((1, 4, nc * width), F32),
        jax.ShapeDtypeStruct((4, H), F32),
        jax.ShapeDtypeStruct((4, H), F32),
        jax.ShapeDtypeStruct((NZ, NX, 8, nc * width), F32),
    )
    results = pl.pallas_call(
        lambda *refs: kernel(nr, *refs),
        out_shape=shapes,
        in_specs=[smem] * 3 + [hbm] * 6,
        out_specs=(hbm,) * 4,
        scratch_shapes=[
            pltpu.VMEM((nc, 2, 4, H), F32),
            pltpu.VMEM((2, 4, H), F32),
            pltpu.VMEM((NZ, NX, 8, nc * width), F32),
            pltpu.VMEM((steps, tokens, rows), BF16),
            pltpu.VMEM((steps, rows, tokens), BF16),
            pltpu.VMEM((nc, rows, width), BF16),
            pltpu.VMEM((nc, rows, width), BF16),
            pltpu.VMEM((nc, 2, NZ, NX, 8, H), F32),
            pltpu.VMEM((nc, NZ, NX, 8, H), F32),
            pltpu.VMEM((nc, NX - 1, NZ, 8, H), F32),
            pltpu.VMEM((nc, NZ, 8, H), F32),
            pltpu.VMEM((nc, NZ - 1, 8, H), F32),
            pltpu.VMEM((nc, nr // 2, 2, 8, H), F32),
            pltpu.VMEM((nr, 8, H), F32),
            pltpu.VMEM((nr, 8, H), F32),
            pltpu.VMEM((nc, NZ, 8, H), F32),
            pltpu.VMEM((nr // 4, 2, 2, 2, 4, H), F32),
            pltpu.VMEM((nr // 4, 2, 2, 4, H), F32),
            pltpu.VMEM((nc, 4, H), F32),
            pltpu.VMEM((nc, 4, H), F32),
            pltpu.VMEM((nc, 4, H), F32),
            pltpu.VMEM((2, 4, H), F32),
            dma,
            dma((nc,)),
            dma((nc,)),
            dma((nc,)),
            dma((2,)),
            dma((8, nc)),
            dma((8, nc)),
            dma((4,)),
            dma((4,)),
            dma((2, nc)),
            dma((2, nc)),
            dma((3, nc)),
        ],
        compiler_params=pltpu.CompilerParams(
            collective_id=0, has_side_effects=True, vmem_limit_bytes=60 * 2**20
        ),
        cost_estimate=pl.CostEstimate(flops=3300000000, bytes_accessed=5000000, transcendentals=4000000),
        name="outer_step",
    )(
        staleness,
        arrival_order,
        pull_slot,
        inputs,
        teacher,
        worker_start,
        regional_momentum,
        global_params,
        global_momentum,
    )
    out_mom, out_par, out_gmom, out_wp = pl.pallas_call(
        hand_on,
        out_shape=shapes,
        in_specs=[hbm] * 4,
        out_specs=(hbm,) * 4,
        scratch_shapes=[pltpu.VMEM(shape.shape, F32) for shape in shapes] + [dma((NZ + 3,)), dma((NZ + 3,))],
        compiler_params=pltpu.CompilerParams(vmem_limit_bytes=60 * 2**20),
        name="hand_on",
    )(*results)
    return out_mom, out_par, out_gmom, out_wp.reshape(1, rows, nc * width)


def solution(mesh):
    nr = mesh.shape["region"]
    placed = (
        P("region", None, None),
        P("region", "worker", None, None, None),
        P(),
        P("region", "worker", None),
        P("worker", "region"),
        P("worker", "region"),
        P(),
        P(),
        P(),
    )
    return jax.shard_map(
        lambda *args: local(nr, *args),
        mesh=mesh,
        in_specs=placed,
        out_specs=(
            P("region", "worker", None),
            P("worker", "region"),
            P("worker", "region"),
            P("region", None, None),
        ),
        check_vma=False,
    )
```

```python
import jax
import jax.numpy as jnp
from jax import lax
from jax.experimental import pallas as pl
from jax.experimental.pallas import tpu as pltpu
from jax.sharding import PartitionSpec as P

LOCAL_RATE = 0.3
REGION_BETA = 0.9
REGION_RATE = 1.0
GLOBAL_MU = 0.9
GLOBAL_RATE = 0.7

MESH = pl.DeviceIdType.MESH
F32 = jnp.float32
BF16 = jnp.bfloat16

NZ = 4
NX = 4
H = 256

PACE = 2
LAG_A, LAG_B, LAG_C, LAG_D, LAG_E, LAG_F, LAG_G, LAG_H = 2, 4, 4, 5, 7, 4, 4, 2
A, B, C, D, E, F, G, HH = range(8)


def dot(a, b):
    return jnp.dot(a, b, preferred_element_type=F32)


def kernel(
    nr,
    stale_ref,
    order_ref,
    slot_ref,
    x_hbm,
    t_hbm,
    w_hbm,
    mom_hbm,
    par_hbm,
    gmom_hbm,
    mom_hout,
    par_hout,
    gmom_hout,
    wp_hout,
    out_mom,
    out_pm,
    out_wp,
    x_v,
    xt_v,
    t_v,
    w_v,
    s_all,
    r_a,
    r_b,
    s_c,
    r_c,
    d_all,
    d_now,
    weights,
    f_all,
    pm_all,
    pm_oth,
    mo_own,
    mo_oth,
    mo_send,
    g_send,
    x_sem,
    t_sem,
    w_sem,
    mo_sem,
    pm_sem,
    send,
    recv,
    misc_send,
    misc_recv,
    mo_ssem,
    mo_rsem,
    out_sem,
):
    nc = nr // 2
    ny = nr // 2
    steps, tokens, _ = x_v.shape
    scale = LOCAL_RATE / tokens
    workers = NZ * NX * 2
    r = lax.axis_index("region")
    w = lax.axis_index("worker")
    z = w // (NX * 2)
    x = (w // 2) % NX
    c = w % 2

    def wid(zz, xx, cc):
        return (zz * NX + xx) * 2 + cc

    partner = {"worker": wid(z, x, 1 - c)}
    x_of = [(x + i) % NX for i in range(NX)]
    z_of = [(z + i) % NZ for i in range(NZ)]
    x_peer = [{"worker": wid(z, x_of[i], c)} for i in range(NX)]
    z_peer = [{"worker": wid(z_of[i], x, c)} for i in range(NZ)]
    hi = r // ny
    y = r % ny
    hi_peer = {"region": (1 - hi) * ny + y}
    y_peer = [{"region": hi * ny + (y + i) % ny} for i in range(ny)]

    barrier = pltpu.get_barrier_semaphore()
    peers = [partner, hi_peer] + x_peer[1:] + z_peer[1:] + y_peer[1:]
    for peer in peers:
        pl.semaphore_signal(barrier, inc=1, device_id=peer, device_id_type=MESH)

    def put(src, dst, s_sem, r_sem, peer):
        pltpu.make_async_remote_copy(
            src_ref=src, dst_ref=dst, send_sem=s_sem, recv_sem=r_sem, device_id=peer, device_id_type=MESH
        ).start()

    def take(ref, sem):
        pltpu.make_async_copy(ref, ref, sem).wait()

    pltpu.make_async_copy(x_hbm.at[0, 0], x_v, x_sem).start()
    for k in range(nc):
        cols = pl.ds(k * 2 * H, 2 * H)
        pltpu.make_async_copy(t_hbm.at[:, cols], t_v.at[k], t_sem.at[k]).start()
        pltpu.make_async_copy(w_hbm.at[0, :, cols], w_v.at[k], w_sem.at[k]).start()
    for k in range(nc):
        mine = pl.ds(pl.multiple_of((2 * k + c) * H, H), H)
        pltpu.make_async_copy(mom_hbm.at[0, :, mine], mo_own.at[k], mo_sem.at[k]).start()
    pltpu.make_async_copy(par_hbm, pm_all.at[0, 0, 0, 0], pm_sem.at[0]).start()
    pltpu.make_async_copy(gmom_hbm, pm_all.at[0, 0, 0, 1], pm_sem.at[1]).start()

    pltpu.make_async_copy(x_hbm.at[0, 0], x_v, x_sem).wait()
    for s in range(steps):
        xt_v[s] = x_v[s].T
    for i in range(nr):
        weights[i] = 1.0 / (1.0 + jnp.full((8, H), stale_ref[i].astype(F32)))

    def tile(k):
        teach = t_v[k].T
        start = w_v[k].T.astype(F32)
        now = start
        for s in range(steps):
            v = dot(teach, xt_v[s])
            predicted = dot(now.astype(BF16), xt_v[s])
            residual = (predicted - v * jax.nn.sigmoid(v)).astype(BF16)
            now = now - scale * dot(residual, x_v[s])
        return (start - now).T

    def compute(k):
        cols = pl.ds(0, 2 * H)
        pltpu.make_async_copy(t_hbm.at[:, cols], t_v.at[k], t_sem.at[k]).wait()
        pltpu.make_async_copy(w_hbm.at[0, :, cols], w_v.at[k], w_sem.at[k]).wait()
        pseudo = tile(k)
        for half in range(2):
            s_all[k, half] = pseudo[:, half * H : half * H + H].reshape(NZ, NX, 8, H)

    def send_a(k):
        put(s_all.at[k, 1 - c], r_a.at[k], send.at[A, k], recv.at[A, k], partner)

    def opening():
        pl.semaphore_wait(barrier, len(peers))
        put(par_hbm, pm_all.at[0, 0, 1, 0], misc_send.at[0], misc_recv.at[0], hi_peer)
        put(gmom_hbm, pm_all.at[0, 0, 1, 1], misc_send.at[0], misc_recv.at[0], hi_peer)
        for k in range(nc):
            theirs = pl.ds(pl.multiple_of((2 * k + 1 - c) * H, H), H)
            put(mom_hbm.at[0, :, theirs], mo_oth.at[k], mo_ssem.at[0, k], mo_rsem.at[0, k], partner)

    def stage_b(k):
        take(r_a.at[k], recv.at[A, k])
        s_all[k, c] = s_all[k, c] + r_a[k]
        for i in (2, 1, 3):
            put(s_all.at[k, c, :, x_of[i]], r_b.at[k, i - 1], send.at[B, k], recv.at[B, k], x_peer[i])

    def stage_c(k):
        take(r_b.at[k], recv.at[B, k])
        total = s_all[k, c, :, x]
        for i in range(NX - 1):
            total = total + r_b[k, i]
        s_c[k] = total
        for i in (2, 3, 1):
            put(s_c.at[k, z_of[i]], r_c.at[k, i - 1], send.at[C, k], recv.at[C, k], z_peer[i])

    def both(mine, other):
        low = jnp.where(c == 0, mine, other)
        high = jnp.where(c == 0, other, mine)
        return jnp.concatenate([low, high], axis=0)

    def parts(value):
        low, high = value[:4], value[4:]
        return jnp.where(c == 0, low, high), jnp.where(c == 0, high, low)

    def columns(k):
        return pl.ds(pl.multiple_of((2 * k + c) * H, H), H)

    def stage_d(k):
        take(mo_own.at[k], mo_sem.at[k])
        take(mo_oth.at[k], mo_rsem.at[0, k])
        take(r_c.at[k], recv.at[C, k])
        summed = s_c[k, z]
        for i in range(NZ - 1):
            summed = summed + r_c[k, i]
        momentum = REGION_BETA * both(mo_own[k], mo_oth[k]) + summed / workers
        d_all[k, 0, 0] = REGION_RATE * momentum
        put(d_all.at[k, 0, 0], d_all.at[k, 0, 1], send.at[D, k], recv.at[D, k], hi_peer)
        mine, other = parts(momentum)
        out_mom[k, c] = mine
        mo_send[k] = other
        put(mo_send.at[k], out_mom.at[k, c], mo_ssem.at[1, k], mo_rsem.at[1, k], partner)

    def stage_e(k):
        take(d_all.at[k, 0, 1], recv.at[D, k])
        for i in (4, 3, 5, 2, 6, 1, 7):
            put(d_all.at[k, 0], d_all.at[k, i], send.at[E, k], recv.at[E, k], y_peer[i])

    def spread():
        take(par_hbm, pm_sem.at[0])
        take(gmom_hbm, pm_sem.at[1])
        take(pm_all.at[0, 0, 1], misc_recv.at[0])
        for i in range(1, ny):
            put(pm_all.at[0, 0], pm_all.at[i // 2, i % 2], misc_send.at[1], misc_recv.at[1], y_peer[i])

    def exchange():
        take(d_all.at[0, pl.ds(1, ny - 1)], misc_recv.at[1])
        put(pm_all.at[:, (y + 1 - c) % 2], pm_oth, misc_send.at[2], misc_recv.at[2], partner)

    def stage_f(k):
        take(d_all.at[k, pl.ds(1, ny - 1)], recv.at[E, k])
        for i in range(ny):
            for h in range(2):
                source = ((hi + h) % 2) * ny + (y - i + ny) % ny
                d_now[source] = weights[source] * d_all[k, i, h]
        owner = 2 * k + c
        away = (y - owner % ny + ny) % ny
        side = (owner // ny + hi) % 2
        params = both(pm_all[away // 2, away % 2, side, 0], pm_oth[away // 2, side, 0])
        momentum = both(pm_all[away // 2, away % 2, side, 1], pm_oth[away // 2, side, 1])
        slot = slot_ref[r]
        pulled = params
        for arrival in range(nr):
            update = d_now[order_ref[arrival]]
            momentum = GLOBAL_MU * momentum + update
            params = params - GLOBAL_RATE * (update + GLOBAL_MU * momentum)
            pulled = jnp.where(slot == arrival, params, pulled)
        f_all[k, z] = pulled
        for i in (2, 3, 1):
            put(f_all.at[k, z], f_all.at[k, z], send.at[F, k], recv.at[F, k], z_peer[i])

        @pl.when(2 * k + c == r)
        def _():
            for i, value in enumerate((params, momentum)):
                mine, other = parts(value)
                out_pm[i] = mine
                g_send[i] = other
            put(g_send, out_pm, misc_send.at[3], misc_recv.at[3], partner)

    def stage_g(k):
        take(f_all.at[k, pl.ds(0, NZ - 1)], recv.at[F, k])
        out_wp[:, x, :, columns(k)] = f_all[k]
        for i in (2, 1, 3):
            put(f_all.at[k], out_wp.at[:, x, :, columns(k)], send.at[G, k], recv.at[G, k], x_peer[i])

    def stage_h(k):
        take(r_b.at[k], recv.at[G, k])
        put(out_wp.at[:, :, :, columns(k)], out_wp.at[:, :, :, columns(k)], send.at[HH, k], recv.at[HH, k], partner)

    def stage_end(k):
        take(r_a.at[k], recv.at[HH, k])
        take(mo_oth.at[k], mo_rsem.at[1, k])
        chunk = pl.ds(pl.multiple_of(2 * k * H, 2 * H), 2 * H)
        pltpu.make_async_copy(out_wp.at[:, :, :, chunk], wp_hout.at[:, :, :, chunk], out_sem.at[0, k]).start()
        for i in range(2):
            half = pl.ds(pl.multiple_of((2 * k + i) * H, H), H)
            pltpu.make_async_copy(out_mom.at[k, i], mom_hout.at[0, :, half], out_sem.at[1 + i, k]).start()
        take(r_a.at[k], send.at[A, k])
        take(r_b.at[k], send.at[B, k])
        take(r_c.at[k], send.at[C, k])
        take(d_all.at[k, 0, 1], send.at[D, k])
        take(d_all.at[k, pl.ds(1, ny - 1)], send.at[E, k])
        take(f_all.at[k, pl.ds(0, NZ - 1)], send.at[F, k])
        take(r_b.at[k], send.at[G, k])
        take(r_a.at[k], send.at[HH, k])
        take(mo_oth.at[k], mo_ssem.at[0, k])
        take(mo_oth.at[k], mo_ssem.at[1, k])

    at_b = LAG_A
    at_c = at_b + LAG_B
    at_d = at_c + LAG_C
    at_e = at_d + LAG_D
    at_f = at_e + LAG_E
    at_g = at_f + LAG_F
    at_h = at_g + LAG_G
    at_end = at_h + LAG_H

    def tick(t, _):
        def when(lag, stage):
            @pl.when((t >= lag) & (t < PACE * nc + lag) & ((t - lag) % PACE == 0))
            def _():
                stage((t - lag) // PACE)

        when(0, compute)
        pl.when(t == 0)(opening)
        when(0, send_a)
        when(at_end, stage_end)
        when(at_h, stage_h)
        when(at_g, stage_g)
        pl.when(t == 8)(spread)
        pl.when(t == at_f - 3)(exchange)

        @pl.when(t == at_f)
        def _():
            take(pm_oth, misc_recv.at[2])

        when(at_f, stage_f)
        when(at_e, stage_e)
        when(at_d, stage_d)
        when(at_c, stage_c)
        when(at_b, stage_b)
        return 0

    lax.fori_loop(0, PACE * (nc - 1) + at_end + 1, tick, 0)
    take(pm_all.at[0, 0, 1], misc_send.at[0])
    take(d_all.at[0, pl.ds(1, ny - 1)], misc_send.at[1])
    take(pm_oth, misc_send.at[2])

    @pl.when(r % 2 == c)
    def _():
        take(g_send, misc_send.at[3])

    @pl.when(r % 2 != c)
    def _():
        take(g_send, misc_recv.at[3])

    pltpu.make_async_copy(out_pm.at[0], par_hout, pm_sem.at[0]).start()
    pltpu.make_async_copy(out_pm.at[1], gmom_hout, pm_sem.at[1]).start()

    def written(k, _):
        take(out_wp.at[:, :, :, pl.ds(0, 2 * H)], out_sem.at[0, k])
        take(mo_send.at[k], out_sem.at[1, k])
        take(mo_send.at[k], out_sem.at[2, k])
        return 0

    lax.fori_loop(0, nc, written, 0)
    take(out_pm.at[0], pm_sem.at[0])
    take(out_pm.at[1], pm_sem.at[1])


def hand_on(*refs):
    given, made, held, arrive, leave = refs[:4], refs[4:8], refs[8:12], refs[12], refs[13]
    routes = [(given[3].at[i], held[3].at[i], made[3].at[i]) for i in range(NZ)]
    routes += [(given[i], held[i], made[i]) for i in range(3)]
    inward = [pltpu.make_async_copy(src, mid, arrive.at[i]) for i, (src, mid, _) in enumerate(routes)]
    outward = [pltpu.make_async_copy(mid, dst, leave.at[i]) for i, (_, mid, dst) in enumerate(routes)]
    for copy in inward:
        copy.start()
    for copy, onward in zip(inward, outward):
        copy.wait()
        onward.start()
    for copy in outward:
        copy.wait()


def local(nr, worker_start, inputs, teacher, regional_momentum, global_params, global_momentum, staleness, arrival_order, pull_slot):
    _, _, steps, tokens, rows = inputs.shape
    nc = nr // 2
    width = 2 * H
    smem = pl.BlockSpec(memory_space=pltpu.SMEM)
    hbm = pl.BlockSpec(memory_space=pltpu.HBM)
    dma = pltpu.SemaphoreType.DMA
    shapes = (
        jax.ShapeDtypeStruct((1, 4, nc * width), F32),
        jax.ShapeDtypeStruct((4, H), F32),
        jax.ShapeDtypeStruct((4, H), F32),
        jax.ShapeDtypeStruct((NZ, NX, 8, nc * width), F32),
    )
    results = pl.pallas_call(
        lambda *refs: kernel(nr, *refs),
        out_shape=shapes,
        in_specs=[smem] * 3 + [hbm] * 6,
        out_specs=(hbm,) * 4,
        scratch_shapes=[
            pltpu.VMEM((nc, 2, 4, H), F32),
            pltpu.VMEM((2, 4, H), F32),
            pltpu.VMEM((NZ, NX, 8, nc * width), F32),
            pltpu.VMEM((steps, tokens, rows), BF16),
            pltpu.VMEM((steps, rows, tokens), BF16),
            pltpu.VMEM((nc, rows, width), BF16),
            pltpu.VMEM((nc, rows, width), BF16),
            pltpu.VMEM((nc, 2, NZ, NX, 8, H), F32),
            pltpu.VMEM((nc, NZ, NX, 8, H), F32),
            pltpu.VMEM((nc, NX - 1, NZ, 8, H), F32),
            pltpu.VMEM((nc, NZ, 8, H), F32),
            pltpu.VMEM((nc, NZ - 1, 8, H), F32),
            pltpu.VMEM((nc, nr // 2, 2, 8, H), F32),
            pltpu.VMEM((nr, 8, H), F32),
            pltpu.VMEM((nr, 8, H), F32),
            pltpu.VMEM((nc, NZ, 8, H), F32),
            pltpu.VMEM((nr // 4, 2, 2, 2, 4, H), F32),
            pltpu.VMEM((nr // 4, 2, 2, 4, H), F32),
            pltpu.VMEM((nc, 4, H), F32),
            pltpu.VMEM((nc, 4, H), F32),
            pltpu.VMEM((nc, 4, H), F32),
            pltpu.VMEM((2, 4, H), F32),
            dma,
            dma((nc,)),
            dma((nc,)),
            dma((nc,)),
            dma((2,)),
            dma((8, nc)),
            dma((8, nc)),
            dma((4,)),
            dma((4,)),
            dma((2, nc)),
            dma((2, nc)),
            dma((3, nc)),
        ],
        compiler_params=pltpu.CompilerParams(
            collective_id=0, has_side_effects=True, vmem_limit_bytes=60 * 2**20
        ),
        cost_estimate=pl.CostEstimate(flops=3300000000, bytes_accessed=5000000, transcendentals=4000000),
        name="outer_step",
    )(
        staleness,
        arrival_order,
        pull_slot,
        inputs,
        teacher,
        worker_start,
        regional_momentum,
        global_params,
        global_momentum,
    )
    out_mom, out_par, out_gmom, out_wp = pl.pallas_call(
        hand_on,
        out_shape=shapes,
        in_specs=[hbm] * 4,
        out_specs=(hbm,) * 4,
        scratch_shapes=[pltpu.VMEM(shape.shape, F32) for shape in shapes] + [dma((NZ + 3,)), dma((NZ + 3,))],
        compiler_params=pltpu.CompilerParams(vmem_limit_bytes=60 * 2**20),
        name="hand_on",
    )(*results)
    return out_mom, out_par, out_gmom, out_wp.reshape(1, rows, nc * width)


def solution(mesh):
    nr = mesh.shape["region"]
    placed = (
        P("region", None, None),
        P("region", "worker", None, None, None),
        P(),
        P("region", "worker", None),
        P("worker", "region"),
        P("worker", "region"),
        P(),
        P(),
        P(),
    )
    return jax.shard_map(
        lambda *args: local(nr, *args),
        mesh=mesh,
        in_specs=placed,
        out_specs=(
            P("region", "worker", None),
            P("worker", "region"),
            P("worker", "region"),
            P("region", None, None),
        ),
        check_vma=False,
    )
```

```python
import jax
import jax.numpy as jnp
from jax import lax
from jax.experimental import pallas as pl
from jax.experimental.pallas import tpu as pltpu
from jax.sharding import PartitionSpec as P

LOCAL_RATE = 0.3
REGION_BETA = 0.9
REGION_RATE = 1.0
GLOBAL_MU = 0.9
GLOBAL_RATE = 0.7

MESH = pl.DeviceIdType.MESH
F32 = jnp.float32
BF16 = jnp.bfloat16

NZ = 4
NX = 4
H = 256

PACE = 2
LAG_A, LAG_B, LAG_C, LAG_D, LAG_E, LAG_F, LAG_G, LAG_H = 2, 4, 4, 5, 7, 4, 4, 2
A, B, C, D, E, F, G, HH = range(8)


def dot(a, b):
    return jnp.dot(a, b, preferred_element_type=F32)


def kernel(
    nr,
    stale_ref,
    order_ref,
    slot_ref,
    x_hbm,
    t_hbm,
    w_hbm,
    mom_hbm,
    par_hbm,
    gmom_hbm,
    mom_hout,
    par_hout,
    gmom_hout,
    wp_hout,
    out_mom,
    out_pm,
    out_wp,
    x_v,
    xt_v,
    t_v,
    w_v,
    s_all,
    r_a,
    r_b,
    s_c,
    r_c,
    d_all,
    d_now,
    weights,
    f_all,
    pm_all,
    pm_oth,
    mo_own,
    mo_oth,
    mo_send,
    g_send,
    x_sem,
    t_sem,
    w_sem,
    mo_sem,
    pm_sem,
    send,
    recv,
    misc_send,
    misc_recv,
    mo_ssem,
    mo_rsem,
    out_sem,
):
    nc = nr // 2
    ny = nr // 2
    steps, tokens, _ = x_v.shape
    scale = LOCAL_RATE / tokens
    workers = NZ * NX * 2
    r = lax.axis_index("region")
    w = lax.axis_index("worker")
    z = w // (NX * 2)
    x = (w // 2) % NX
    c = w % 2

    def wid(zz, xx, cc):
        return (zz * NX + xx) * 2 + cc

    partner = {"worker": wid(z, x, 1 - c)}
    x_of = [(x + i) % NX for i in range(NX)]
    z_of = [(z + i) % NZ for i in range(NZ)]
    x_peer = [{"worker": wid(z, x_of[i], c)} for i in range(NX)]
    z_peer = [{"worker": wid(z_of[i], x, c)} for i in range(NZ)]
    hi = r // ny
    y = r % ny
    hi_peer = {"region": (1 - hi) * ny + y}
    y_peer = [{"region": hi * ny + (y + i) % ny} for i in range(ny)]

    barrier = pltpu.get_barrier_semaphore()
    peers = [partner, hi_peer] + x_peer[1:] + z_peer[1:] + y_peer[1:]
    def put(src, dst, s_sem, r_sem, peer):
        pltpu.make_async_remote_copy(
            src_ref=src, dst_ref=dst, send_sem=s_sem, recv_sem=r_sem, device_id=peer, device_id_type=MESH
        ).start()

    def take(ref, sem):
        pltpu.make_async_copy(ref, ref, sem).wait()

    pltpu.make_async_copy(x_hbm.at[0, 0], x_v, x_sem).start()
    for k in range(nc):
        cols = pl.ds(k * 2 * H, 2 * H)
        pltpu.make_async_copy(t_hbm.at[:, cols], t_v.at[k], t_sem.at[k]).start()
        pltpu.make_async_copy(w_hbm.at[0, :, cols], w_v.at[k], w_sem.at[k]).start()
    for peer in peers:
        pl.semaphore_signal(barrier, inc=1, device_id=peer, device_id_type=MESH)

    for k in range(nc):
        mine = pl.ds(pl.multiple_of((2 * k + c) * H, H), H)
        pltpu.make_async_copy(mom_hbm.at[0, :, mine], mo_own.at[k], mo_sem.at[k]).start()
    pltpu.make_async_copy(par_hbm, pm_all.at[0, 0, 0, 0], pm_sem.at[0]).start()
    pltpu.make_async_copy(gmom_hbm, pm_all.at[0, 0, 0, 1], pm_sem.at[1]).start()

    pltpu.make_async_copy(x_hbm.at[0, 0], x_v, x_sem).wait()
    for s in range(steps):
        xt_v[s] = x_v[s].T
    for i in range(nr):
        weights[i] = 1.0 / (1.0 + jnp.full((8, H), stale_ref[i].astype(F32)))

    def tile(k):
        teach = t_v[k].T
        start = w_v[k].T.astype(F32)
        now = start
        for s in range(steps):
            v = dot(teach, xt_v[s])
            predicted = dot(now.astype(BF16), xt_v[s])
            residual = (predicted - v * jax.nn.sigmoid(v)).astype(BF16)
            now = now - scale * dot(residual, x_v[s])
        return (start - now).T

    def compute(k):
        cols = pl.ds(0, 2 * H)
        pltpu.make_async_copy(t_hbm.at[:, cols], t_v.at[k], t_sem.at[k]).wait()
        pltpu.make_async_copy(w_hbm.at[0, :, cols], w_v.at[k], w_sem.at[k]).wait()
        pseudo = tile(k)
        for half in range(2):
            s_all[k, half] = pseudo[:, half * H : half * H + H].reshape(NZ, NX, 8, H)

    def send_a(k):
        put(s_all.at[k, 1 - c], r_a.at[k], send.at[A, k], recv.at[A, k], partner)

    def opening():
        pl.semaphore_wait(barrier, len(peers))
        put(par_hbm, pm_all.at[0, 0, 1, 0], misc_send.at[0], misc_recv.at[0], hi_peer)
        put(gmom_hbm, pm_all.at[0, 0, 1, 1], misc_send.at[0], misc_recv.at[0], hi_peer)
        for k in range(nc):
            theirs = pl.ds(pl.multiple_of((2 * k + 1 - c) * H, H), H)
            put(mom_hbm.at[0, :, theirs], mo_oth.at[k], mo_ssem.at[0, k], mo_rsem.at[0, k], partner)

    def stage_b(k):
        take(r_a.at[k], recv.at[A, k])
        s_all[k, c] = s_all[k, c] + r_a[k]
        for i in (2, 1, 3):
            put(s_all.at[k, c, :, x_of[i]], r_b.at[k, i - 1], send.at[B, k], recv.at[B, k], x_peer[i])

    def stage_c(k):
        take(r_b.at[k], recv.at[B, k])
        total = s_all[k, c, :, x]
        for i in range(NX - 1):
            total = total + r_b[k, i]
        s_c[k] = total
        for i in (2, 3, 1):
            put(s_c.at[k, z_of[i]], r_c.at[k, i - 1], send.at[C, k], recv.at[C, k], z_peer[i])

    def both(mine, other):
        low = jnp.where(c == 0, mine, other)
        high = jnp.where(c == 0, other, mine)
        return jnp.concatenate([low, high], axis=0)

    def parts(value):
        low, high = value[:4], value[4:]
        return jnp.where(c == 0, low, high), jnp.where(c == 0, high, low)

    def columns(k):
        return pl.ds(pl.multiple_of((2 * k + c) * H, H), H)

    def stage_d(k):
        take(mo_own.at[k], mo_sem.at[k])
        take(mo_oth.at[k], mo_rsem.at[0, k])
        take(r_c.at[k], recv.at[C, k])
        summed = s_c[k, z]
        for i in range(NZ - 1):
            summed = summed + r_c[k, i]
        momentum = REGION_BETA * both(mo_own[k], mo_oth[k]) + summed / workers
        d_all[k, 0, 0] = REGION_RATE * momentum
        put(d_all.at[k, 0, 0], d_all.at[k, 0, 1], send.at[D, k], recv.at[D, k], hi_peer)
        mine, other = parts(momentum)
        out_mom[k, c] = mine
        mo_send[k] = other
        put(mo_send.at[k], out_mom.at[k, c], mo_ssem.at[1, k], mo_rsem.at[1, k], partner)

    def stage_e(k):
        take(d_all.at[k, 0, 1], recv.at[D, k])
        for i in (4, 3, 5, 2, 6, 1, 7):
            put(d_all.at[k, 0], d_all.at[k, i], send.at[E, k], recv.at[E, k], y_peer[i])

    def spread():
        take(par_hbm, pm_sem.at[0])
        take(gmom_hbm, pm_sem.at[1])
        take(pm_all.at[0, 0, 1], misc_recv.at[0])
        for i in range(1, ny):
            put(pm_all.at[0, 0], pm_all.at[i // 2, i % 2], misc_send.at[1], misc_recv.at[1], y_peer[i])

    def exchange():
        take(d_all.at[0, pl.ds(1, ny - 1)], misc_recv.at[1])
        put(pm_all.at[:, (y + 1 - c) % 2], pm_oth, misc_send.at[2], misc_recv.at[2], partner)

    def stage_f(k):
        take(d_all.at[k, pl.ds(1, ny - 1)], recv.at[E, k])
        for i in range(ny):
            for h in range(2):
                source = ((hi + h) % 2) * ny + (y - i + ny) % ny
                d_now[source] = weights[source] * d_all[k, i, h]
        owner = 2 * k + c
        away = (y - owner % ny + ny) % ny
        side = (owner // ny + hi) % 2
        params = both(pm_all[away // 2, away % 2, side, 0], pm_oth[away // 2, side, 0])
        momentum = both(pm_all[away // 2, away % 2, side, 1], pm_oth[away // 2, side, 1])
        slot = slot_ref[r]
        pulled = params
        for arrival in range(nr):
            update = d_now[order_ref[arrival]]
            momentum = GLOBAL_MU * momentum + update
            params = params - GLOBAL_RATE * (update + GLOBAL_MU * momentum)
            pulled = jnp.where(slot == arrival, params, pulled)
        f_all[k, z] = pulled
        for i in (2, 3, 1):
            put(f_all.at[k, z], f_all.at[k, z], send.at[F, k], recv.at[F, k], z_peer[i])

        @pl.when(2 * k + c == r)
        def _():
            for i, value in enumerate((params, momentum)):
                mine, other = parts(value)
                out_pm[i] = mine
                g_send[i] = other
            put(g_send, out_pm, misc_send.at[3], misc_recv.at[3], partner)

    def stage_g(k):
        take(f_all.at[k, pl.ds(0, NZ - 1)], recv.at[F, k])
        out_wp[:, x, :, columns(k)] = f_all[k]
        for i in (2, 1, 3):
            put(f_all.at[k], out_wp.at[:, x, :, columns(k)], send.at[G, k], recv.at[G, k], x_peer[i])

    def stage_h(k):
        take(r_b.at[k], recv.at[G, k])
        put(out_wp.at[:, :, :, columns(k)], out_wp.at[:, :, :, columns(k)], send.at[HH, k], recv.at[HH, k], partner)

        pltpu.make_async_copy(out_wp.at[:, :, :, columns(k)], wp_hout.at[:, :, :, columns(k)], out_sem.at[3, k]).start()

    def stage_end(k):
        take(r_a.at[k], recv.at[HH, k])
        take(mo_oth.at[k], mo_rsem.at[1, k])
        theirs = pl.ds(pl.multiple_of((2 * k + 1 - c) * H, H), H)
        pltpu.make_async_copy(out_wp.at[:, :, :, theirs], wp_hout.at[:, :, :, theirs], out_sem.at[0, k]).start()
        for i in range(2):
            half = pl.ds(pl.multiple_of((2 * k + i) * H, H), H)
            pltpu.make_async_copy(out_mom.at[k, i], mom_hout.at[0, :, half], out_sem.at[1 + i, k]).start()
        take(r_a.at[k], send.at[A, k])
        take(r_b.at[k], send.at[B, k])
        take(r_c.at[k], send.at[C, k])
        take(d_all.at[k, 0, 1], send.at[D, k])
        take(d_all.at[k, pl.ds(1, ny - 1)], send.at[E, k])
        take(f_all.at[k, pl.ds(0, NZ - 1)], send.at[F, k])
        take(r_b.at[k], send.at[G, k])
        take(r_a.at[k], send.at[HH, k])
        take(mo_oth.at[k], mo_ssem.at[0, k])
        take(mo_oth.at[k], mo_ssem.at[1, k])

    at_b = LAG_A
    at_c = at_b + LAG_B
    at_d = at_c + LAG_C
    at_e = at_d + LAG_D
    at_f = at_e + LAG_E
    at_g = at_f + LAG_F
    at_h = at_g + LAG_G
    at_end = at_h + LAG_H

    def tick(t, _):
        def when(lag, stage):
            @pl.when((t >= lag) & (t < PACE * nc + lag) & ((t - lag) % PACE == 0))
            def _():
                stage((t - lag) // PACE)

        when(0, compute)
        pl.when(t == 0)(opening)
        when(0, send_a)
        when(at_end, stage_end)
        when(at_h, stage_h)
        when(at_g, stage_g)
        pl.when(t == 8)(spread)
        pl.when(t == at_f - 3)(exchange)

        @pl.when(t == at_f)
        def _():
            take(pm_oth, misc_recv.at[2])

        when(at_f, stage_f)
        when(at_e, stage_e)
        when(at_d, stage_d)
        when(at_c, stage_c)
        when(at_b, stage_b)
        return 0

    lax.fori_loop(0, PACE * (nc - 1) + at_end + 1, tick, 0)
    take(pm_all.at[0, 0, 1], misc_send.at[0])
    take(d_all.at[0, pl.ds(1, ny - 1)], misc_send.at[1])
    take(pm_oth, misc_send.at[2])

    @pl.when(r % 2 == c)
    def _():
        take(g_send, misc_send.at[3])

    @pl.when(r % 2 != c)
    def _():
        take(g_send, misc_recv.at[3])

    pltpu.make_async_copy(out_pm.at[0], par_hout, pm_sem.at[0]).start()
    pltpu.make_async_copy(out_pm.at[1], gmom_hout, pm_sem.at[1]).start()

    def written(k, _):
        take(r_a.at[k], out_sem.at[0, k])
        take(r_a.at[k], out_sem.at[3, k])
        take(mo_send.at[k], out_sem.at[1, k])
        take(mo_send.at[k], out_sem.at[2, k])
        return 0

    lax.fori_loop(0, nc, written, 0)
    take(out_pm.at[0], pm_sem.at[0])
    take(out_pm.at[1], pm_sem.at[1])


def hand_on(*refs):
    given, made, held, arrive, leave = refs[:4], refs[4:8], refs[8:12], refs[12], refs[13]
    routes = [(given[3].at[i], held[3].at[i], made[3].at[i]) for i in range(NZ)]
    routes += [(given[i], held[i], made[i]) for i in range(3)]
    inward = [pltpu.make_async_copy(src, mid, arrive.at[i]) for i, (src, mid, _) in enumerate(routes)]
    outward = [pltpu.make_async_copy(mid, dst, leave.at[i]) for i, (_, mid, dst) in enumerate(routes)]
    for copy in inward:
        copy.start()
    for copy, onward in zip(inward, outward):
        copy.wait()
        onward.start()
    for copy in outward:
        copy.wait()


def local(nr, worker_start, inputs, teacher, regional_momentum, global_params, global_momentum, staleness, arrival_order, pull_slot):
    _, _, steps, tokens, rows = inputs.shape
    nc = nr // 2
    width = 2 * H
    smem = pl.BlockSpec(memory_space=pltpu.SMEM)
    hbm = pl.BlockSpec(memory_space=pltpu.HBM)
    dma = pltpu.SemaphoreType.DMA
    shapes = (
        jax.ShapeDtypeStruct((1, 4, nc * width), F32),
        jax.ShapeDtypeStruct((4, H), F32),
        jax.ShapeDtypeStruct((4, H), F32),
        jax.ShapeDtypeStruct((NZ, NX, 8, nc * width), F32),
    )
    results = pl.pallas_call(
        lambda *refs: kernel(nr, *refs),
        out_shape=shapes,
        in_specs=[smem] * 3 + [hbm] * 6,
        out_specs=(hbm,) * 4,
        scratch_shapes=[
            pltpu.VMEM((nc, 2, 4, H), F32),
            pltpu.VMEM((2, 4, H), F32),
            pltpu.VMEM((NZ, NX, 8, nc * width), F32),
            pltpu.VMEM((steps, tokens, rows), BF16),
            pltpu.VMEM((steps, rows, tokens), BF16),
            pltpu.VMEM((nc, rows, width), BF16),
            pltpu.VMEM((nc, rows, width), BF16),
            pltpu.VMEM((nc, 2, NZ, NX, 8, H), F32),
            pltpu.VMEM((nc, NZ, NX, 8, H), F32),
            pltpu.VMEM((nc, NX - 1, NZ, 8, H), F32),
            pltpu.VMEM((nc, NZ, 8, H), F32),
            pltpu.VMEM((nc, NZ - 1, 8, H), F32),
            pltpu.VMEM((nc, nr // 2, 2, 8, H), F32),
            pltpu.VMEM((nr, 8, H), F32),
            pltpu.VMEM((nr, 8, H), F32),
            pltpu.VMEM((nc, NZ, 8, H), F32),
            pltpu.VMEM((nr // 4, 2, 2, 2, 4, H), F32),
            pltpu.VMEM((nr // 4, 2, 2, 4, H), F32),
            pltpu.VMEM((nc, 4, H), F32),
            pltpu.VMEM((nc, 4, H), F32),
            pltpu.VMEM((nc, 4, H), F32),
            pltpu.VMEM((2, 4, H), F32),
            dma,
            dma((nc,)),
            dma((nc,)),
            dma((nc,)),
            dma((2,)),
            dma((8, nc)),
            dma((8, nc)),
            dma((4,)),
            dma((4,)),
            dma((2, nc)),
            dma((2, nc)),
            dma((4, nc)),
        ],
        compiler_params=pltpu.CompilerParams(
            collective_id=0, has_side_effects=True, vmem_limit_bytes=60 * 2**20
        ),
        cost_estimate=pl.CostEstimate(flops=3300000000, bytes_accessed=5000000, transcendentals=4000000),
        name="outer_step",
    )(
        staleness,
        arrival_order,
        pull_slot,
        inputs,
        teacher,
        worker_start,
        regional_momentum,
        global_params,
        global_momentum,
    )
    out_mom, out_par, out_gmom, out_wp = pl.pallas_call(
        hand_on,
        out_shape=shapes,
        in_specs=[hbm] * 4,
        out_specs=(hbm,) * 4,
        scratch_shapes=[pltpu.VMEM(shape.shape, F32) for shape in shapes] + [dma((NZ + 3,)), dma((NZ + 3,))],
        compiler_params=pltpu.CompilerParams(vmem_limit_bytes=60 * 2**20),
        name="hand_on",
    )(*results)
    return out_mom, out_par, out_gmom, out_wp.reshape(1, rows, nc * width)


def solution(mesh):
    nr = mesh.shape["region"]
    placed = (
        P("region", None, None),
        P("region", "worker", None, None, None),
        P(),
        P("region", "worker", None),
        P("worker", "region"),
        P("worker", "region"),
        P(),
        P(),
        P(),
    )
    return jax.shard_map(
        lambda *args: local(nr, *args),
        mesh=mesh,
        in_specs=placed,
        out_specs=(
            P("region", "worker", None),
            P("worker", "region"),
            P("worker", "region"),
            P("region", None, None),
        ),
        check_vma=False,
    )
```
